512 devices in a mesh: space: 8 (over y, core), energy: 64 (over x, z).
Axes of the slice: x: 4, y: 4, z: 16, core: 2. Of those that a mesh axis runs over, the one named last changes fastest.
Arguments:
- green_lesser: bfloat16 [64, 8, 2, 256, 256], P('energy', 'space'), may hold values from -6 to 6
- screened_lesser: bfloat16 [64, 8, 2, 256, 256], P('energy', 'space'), may hold values from -0.75 to 0.75
- green_retarded: bfloat16 [64, 8, 2, 256, 256], P('energy', 'space'), may hold values from -6 to 6
- screened_retarded: bfloat16 [64, 8, 2, 256, 256], P('energy', 'space'), may hold values from -0.75 to 0.75
- left_green: bfloat16 [64, 8, 2, 256, 256], P('energy', 'space'), may hold values from -0.25 to 0.25
- coupling: bfloat16 [8, 2, 256, 256], P('space'), may hold values from -0.25 to 0.25
Outputs:
- lesser_left: bfloat16 [64, 8, 2, 256, 256], P('energy', 'space')
- sigma_retarded: bfloat16 [64, 8, 2, 256, 256], P('energy', 'space')
The draws below stay inside these ranges and needn't reach their ends.
All inputs are finite; a program needn't handle non-finite values.
Results may differ from the reference program's by a relative error of at most 0.018.
Values may be sent and summed in bfloat16 or wider, within the bound.
A program may use at most 64 MiB of HBM per device.

```python
import jax
import jax.numpy as jnp
from jax import lax

B = 256
NE = 64
NSLAB = 8


def steps_of(rng, dims, pieces, low, largest):
    def one(position, parts):
        draws = jax.random.uniform(jax.random.fold_in(jax.random.fold_in(rng, 6), position), (parts,), jnp.float32, low / len(pieces), largest / len(pieces))
        return jnp.repeat(jnp.exp(draws), dims[position] // parts).reshape((-1,) + (1,) * (len(dims) - position - 1))

    factor_of = one(*pieces[0])
    for cut in pieces[1:]:
        factor_of = factor_of * one(*cut)
    return factor_of


def gaussian(key, shape, scale, reach, pieces=(), kind=jnp.bfloat16):
    values = jax.random.normal(key, shape, jnp.float32) * scale
    if len(pieces) > 0:
        values = steps_of(key, shape, pieces, -0.22, 0.18) * values
    return jnp.clip(values, min=-reach, max=reach).astype(kind)


def setup_inputs(seed: int = 0) -> dict:
    key_list = jax.random.split(jax.random.key(seed), 7)
    return {
        "green_lesser": gaussian(key_list[0], (NE, NSLAB, 2, B, B), 1.0, 6.0, ((0, 64), (1, 8))),
        "screened_lesser": gaussian(key_list[1], (NE, NSLAB, 2, B, B), NE ** -0.5, 0.75, ((0, 64), (1, 8))),
        "green_retarded": gaussian(key_list[2], (NE, NSLAB, 2, B, B), 1.0, 6.0, ((0, 64), (1, 8))),
        "screened_retarded": gaussian(key_list[3], (NE, NSLAB, 2, B, B), NE ** -0.5, 0.75, ((0, 64), (1, 8))),
        "left_green": gaussian(key_list[4], (NE, NSLAB, 2, B, B), (2 * B) ** -0.5, 0.25, ((0, 64), (1, 8))),
        "coupling": gaussian(key_list[5], (NSLAB, 2, B, B), (2 * B) ** -0.5, 0.25, ((0, 8),)),
    }


def contract(einsum_pattern, first_factor, second_factor):
    return jnp.einsum(einsum_pattern, first_factor, second_factor, precision=lax.Precision.HIGHEST, preferred_element_type=jnp.float32)


def complex_product(einsum_pattern, first_factor, second_factor):
    first_real, first_imag = first_factor[..., 0, :, :], first_factor[..., 1, :, :]
    second_real, second_imag = second_factor[..., 0, :, :], second_factor[..., 1, :, :]
    real_part = contract(einsum_pattern, first_real, second_real) - contract(einsum_pattern, first_imag, second_imag)
    imag_part = contract(einsum_pattern, first_real, second_imag) + contract(einsum_pattern, first_imag, second_real)
    return jnp.stack([real_part, imag_part], axis=-3)


def adjoint_product(einsum_pattern, first_factor, second_factor):
    first_real, first_imag = first_factor[..., 0, :, :], first_factor[..., 1, :, :]
    second_real, second_imag = second_factor[..., 0, :, :], second_factor[..., 1, :, :]
    real_part = contract(einsum_pattern, first_real, second_real) + contract(einsum_pattern, first_imag, second_imag)
    imag_part = contract(einsum_pattern, first_imag, second_real) - contract(einsum_pattern, first_real, second_imag)
    return jnp.stack([real_part, imag_part], axis=-3)


def rounded(values):
    return lax.optimization_barrier(values.astype(jnp.bfloat16))


def as_complex(stacked):
    values = stacked.astype(jnp.float32)
    return values[:, 0] + 1j * values[:, 1]


def spectrum_green(stacked):
    values = as_complex(stacked)
    return jnp.fft.fft(jnp.concatenate([values, jnp.zeros_like(values)], axis=0), axis=0)


def spectrum_screen(stacked):
    values = as_complex(stacked)
    middle = NE // 2
    padded = jnp.concatenate([values[middle:], jnp.zeros_like(values), values[:middle]], axis=0)
    return jnp.fft.fft(padded, axis=0)


def back_to_energy(spectrum):
    values = jnp.fft.ifft(spectrum, axis=0)[:NE]
    return jnp.stack([jnp.real(values), jnp.imag(values)], axis=1).astype(jnp.bfloat16)


def reference(green_lesser, screened_lesser, green_retarded, screened_retarded, left_green, coupling):
    def convolve_slab(slab_index):
        def pick(array):
            return lax.dynamic_index_in_dim(array, slab_index, axis=1, keepdims=False)

        green_less = spectrum_green(pick(green_lesser))
        green_ret = spectrum_green(pick(green_retarded))
        screen_less = spectrum_screen(pick(screened_lesser))
        screen_ret = spectrum_screen(pick(screened_retarded))
        lesser_hat = green_less * screen_less
        retarded_hat = green_ret * screen_less + green_less * screen_ret + green_ret * screen_ret
        return back_to_energy(lesser_hat), back_to_energy(retarded_hat)

    slab_numbers = jnp.arange(NSLAB, dtype=jnp.int32)
    sigma_lesser, sigma_ret = lax.map(convolve_slab, slab_numbers)

    def slab_step(state, slab_index):
        green_slab = lax.dynamic_index_in_dim(left_green, slab_index, axis=1, keepdims=False).astype(jnp.float32)
        coupling_slab = lax.dynamic_index_in_dim(coupling, slab_index, axis=0, keepdims=False).astype(jnp.float32)
        sigma_slab = lax.dynamic_index_in_dim(sigma_lesser, slab_index, axis=0, keepdims=False).astype(jnp.float32)
        propagator = rounded(complex_product("nij,jk->nik", green_slab, coupling_slab)).astype(jnp.float32)
        half_source = rounded(complex_product("nij,njk->nik", green_slab, sigma_slab)).astype(jnp.float32)
        source = adjoint_product("nij,nkj->nik", half_source, green_slab)
        inner = complex_product("nij,njk->nik", propagator, state)
        new_state = source + adjoint_product("nij,nkj->nik", inner, propagator)
        return new_state, new_state.astype(jnp.bfloat16)

    initial = jnp.zeros((NE, 2, B, B), jnp.float32)
    _, lesser_left = lax.scan(slab_step, initial, slab_numbers)
    return jnp.moveaxis(lesser_left, 0, 1), jnp.moveaxis(sigma_ret, 0, 1)
```

```python
import functools
import math

import jax
import jax.numpy as jnp
import ml_dtypes
import numpy as np
from jax import lax
from jax.experimental import pallas as pl
from jax.experimental.pallas import tpu as pltpu
from jax.sharding import PartitionSpec as P

MESH = pl.DeviceIdType.MESH
BF16 = jnp.bfloat16
F32 = jnp.float32
NE = 64
LENGTH = 96
LAG = 32


def split_table(table):
    upper = table.astype(ml_dtypes.bfloat16)
    lower = (table - upper.astype(np.float64)).astype(ml_dtypes.bfloat16)
    return np.stack([upper, lower])


def tables():
    step = 2.0 * math.pi / LENGTH
    k = np.arange(LENGTH)
    n = np.arange(NE)
    angle = (k[:, None] * n[None, :] % LENGTH) * step
    forward = np.block([[np.cos(angle), np.sin(angle)], [-np.sin(angle), np.cos(angle)]])
    angle = ((n[:, None] + LAG) * k[None, :] % LENGTH) * step
    back = np.block([[np.cos(angle), -np.sin(angle)], [np.sin(angle), np.cos(angle)]]) / LENGTH
    return split_table(forward), split_table(back)


def dot(first, second):
    return jnp.dot(first, second, preferred_element_type=F32)


def dot_t(first, second):
    return lax.dot_general(first, second, (((1,), (1,)), ((), ())), preferred_element_type=F32)


def product(a_re, a_im, b_re, b_im):
    return dot(a_re, b_re) - dot(a_im, b_im), dot(a_re, b_im) + dot(a_im, b_re)


def adjoint(a_re, a_im, b_re, b_im):
    return dot_t(a_re, b_re) + dot_t(a_im, b_im), dot_t(a_im, b_re) - dot_t(a_re, b_im)


def sandwich(p_ref, s_ref):
    p_re, p_im = p_ref[0], p_ref[1]
    i_re, i_im = product(p_re, p_im, s_ref[0], s_ref[1])
    return adjoint(i_re.astype(BF16), i_im.astype(BF16), p_re, p_im)


def pack(src, dst):
    @pl.loop(0, 16)
    def _(b):
        for cb in range(2):
            re = src[0, pl.ds(16 * b, 16), 128 * cb : 128 * cb + 128].astype(F32)
            im = src[1, pl.ds(16 * b, 16), 128 * cb : 128 * cb + 128].astype(F32)
            for h in range(2):
                both = jnp.concatenate([re[8 * h : 8 * h + 8], im[8 * h : 8 * h + 8]], axis=0)
                dst[4 * b + 2 * h + cb, :, :] = both.astype(BF16)


def unpack(src, dst):
    @pl.loop(0, 16)
    def _(b):
        for cb in range(2):
            low = src[4 * b + cb].astype(F32)
            high = src[4 * b + 2 + cb].astype(F32)
            for part in range(2):
                rows = slice(8 * part, 8 * part + 8)
                both = jnp.concatenate([low[rows], high[rows]], axis=0)
                dst[part, pl.ds(16 * b, 16), 128 * cb : 128 * cb + 128] = both.astype(BF16)


def stage(received, wide):
    @pl.loop(0, 16)
    def _(i):
        wide[pl.ds(64 * i, 64), :] = received[pl.ds(4 * i, 4)].reshape(64, 128).astype(F32)


def gather_columns(wide, q):
    columns = []
    for s in (2 * q, 2 * q + 1):
        re = wide[pl.ds(s, NE, 16), :]
        im = wide[pl.ds(8 + s, NE, 16), :]
        columns.append(jnp.concatenate([re, im], axis=0))
    return jnp.concatenate(columns, axis=1).astype(BF16)


def spectrum(wide, forward, q):
    columns = gather_columns(wide, q)
    both = dot(forward[0], columns) + dot(forward[1], columns)
    return both[:LENGTH], both[LENGTH:]


def times(a, b):
    return a[0] * b[0] - a[1] * b[1], a[0] * b[1] + a[1] * b[0]


def back_to_energy(hat, back, wide, q):
    both = jnp.concatenate(hat, axis=0)
    upper = both.astype(BF16)
    lower = (both - upper.astype(F32)).astype(BF16)
    values = dot(back[0], upper) + dot(back[1], upper) + dot(back[0], lower)
    for i, s in enumerate((2 * q, 2 * q + 1)):
        wide[pl.ds(s, NE, 16), :] = values[:NE, 128 * i : 128 * i + 128]
        wide[pl.ds(8 + s, NE, 16), :] = values[NE:, 128 * i : 128 * i + 128]


def narrow(wide, dst):
    @pl.loop(0, 16)
    def _(i):
        dst[pl.ds(4 * i, 4)] = wide[pl.ds(64 * i, 64), :].reshape(4, 16, 128).astype(BF16)


def kernel(
    gl, wl, gr, wr, lg, cp, fwd, bwd, out_l, out_r,
    s_gl, s_wl, s_gr, s_wr, r_gl, r_wl, r_gr, r_wr, o_l, o_r, q_l, q_r,
    wide_a, wide_b, f_gl, f_wl, f_gr,
    sig, prop, trans, src, half, in_p, in_s, in_e,
    e_send, e_recv, s_send, s_recv,
):
    me = lax.axis_index("energy")
    pos = lax.axis_index("space")
    y, core = pos // 2, pos % 2

    barrier = pltpu.get_barrier_semaphore()

    @pl.loop(1, NE)
    def _(s):
        pl.semaphore_signal(barrier, inc=1, device_id={"energy": lax.rem(me + s, NE)}, device_id_type=MESH)

    @pl.loop(1, 8)
    def _(s):
        pl.semaphore_signal(barrier, inc=1, device_id={"space": lax.rem(pos + s, 8)}, device_id_type=MESH)

    pack(gl, s_gl)
    pack(wl, s_wl)
    pack(gr, s_gr)
    pack(wr, s_wr)
    pl.semaphore_wait(barrier, NE - 1 + 7)

    def exchange(slot, *pairs):
        @pl.loop(1, NE)
        def _(s):
            peer = lax.rem(me + s, NE)
            for i, (source, target) in enumerate(pairs):
                pltpu.make_async_remote_copy(
                    src_ref=source.at[peer],
                    dst_ref=target.at[me],
                    send_sem=e_send.at[slot + i],
                    recv_sem=e_recv.at[slot + i],
                    device_id={"energy": peer},
                    device_id_type=MESH,
                ).start()

        for source, target in pairs:
            target[me] = source[me]

    def wait_recv(slot, buffer):
        pltpu.make_async_copy(buffer.at[pl.ds(0, NE - 1)], buffer.at[pl.ds(0, NE - 1)], e_recv.at[slot]).wait()

    def wait_send(slot, buffer):
        pltpu.make_async_copy(buffer.at[pl.ds(0, NE - 1)], buffer.at[pl.ds(0, NE - 1)], e_send.at[slot]).wait()

    def to_space(slot, source, target, where):
        return pltpu.make_async_remote_copy(
            src_ref=source,
            dst_ref=target,
            send_sem=s_send.at[slot],
            recv_sem=s_recv.at[slot],
            device_id={"space": where},
            device_id_type=MESH,
        )

    exchange(0, (s_gl, r_gl), (s_wl, r_wl))
    exchange(2, (s_gr, r_gr))

    p_re, p_im = product(lg[0], lg[1], cp[0], cp[1])
    prop[0] = p_re.astype(BF16)
    prop[1] = p_im.astype(BF16)
    p_over = to_space(0, prop, in_p, lax.rem(pos + 1, 8))

    @pl.when(core == 0)
    def _():
        p_over.start()
        p_over.wait_send()

    @pl.when(core == 1)
    def _():
        p_over.wait_recv()
        t_re, t_im = product(prop[0], prop[1], in_p[0], in_p[1])
        trans[0] = t_re.astype(BF16)
        trans[1] = t_im.astype(BF16)

    wait_recv(0, r_gl)
    wait_recv(1, r_wl)
    stage(r_gl, wide_a)
    stage(r_wl, wide_b)
    for q in range(4):
        f_gl[q, 0], f_gl[q, 1] = spectrum(wide_a, fwd, q)
        f_wl[q, 0], f_wl[q, 1] = spectrum(wide_b, fwd, q)
    for q in range(4):
        hat = times((f_gl[q, 0], f_gl[q, 1]), (f_wl[q, 0], f_wl[q, 1]))
        back_to_energy(hat, bwd, wide_a, q)
    narrow(wide_a, o_l)
    exchange(4, (o_l, q_l))
    exchange(3, (s_wr, r_wr))

    wait_recv(2, r_gr)
    stage(r_gr, wide_a)
    for q in range(4):
        f_gr[q, 0], f_gr[q, 1] = spectrum(wide_a, fwd, q)

    wait_recv(4, q_l)
    unpack(q_l, sig)
    h_re, h_im = product(lg[0], lg[1], sig[0], sig[1])
    half[0] = h_re.astype(BF16)
    half[1] = h_im.astype(BF16)
    src[0], src[1] = adjoint(half[0], half[1], lg[0], lg[1])
    s_over = to_space(1, half, in_s, lax.rem(pos + 1, 8))

    @pl.when(core == 0)
    def _():
        half[0] = src[0].astype(BF16)
        half[1] = src[1].astype(BF16)
        s_over.start()

    @pl.when(core == 1)
    def _():
        s_over.wait_recv()
        a_re, a_im = sandwich(prop, in_s)
        src[0] += a_re
        src[1] += a_im

    def finish_retarded():
        wait_recv(3, r_wr)
        stage(r_wr, wide_b)
        for q in range(4):
            w_r = spectrum(wide_b, fwd, q)
            w_l = (f_wl[q, 0], f_wl[q, 1])
            first = times((f_gr[q, 0], f_gr[q, 1]), (w_l[0] + w_r[0], w_l[1] + w_r[1]))
            second = times((f_gl[q, 0], f_gl[q, 1]), w_r)
            back_to_energy((first[0] + second[0], first[1] + second[1]), bwd, wide_a, q)
        narrow(wide_a, o_r)
        exchange(5, (o_r, q_r))

    finish_retarded()

    e_ahead = to_space(2, out_l, in_e, lax.rem(pos + 2, 8))
    e_beside = to_space(3, in_e, in_e, lax.rem(pos + 7, 8))

    @pl.when(core == 0)
    def _():
        s_over.wait_send()

        @pl.when(y == 0)
        def _():
            out_l[...] = src[...].astype(BF16)

        @pl.when(y > 0)
        def _():
            e_beside.wait_recv()
            a_re, a_im = sandwich(prop, in_e)
            out_l[0] = (src[0] + a_re).astype(BF16)
            out_l[1] = (src[1] + a_im).astype(BF16)

    @pl.when(core == 1)
    def _():
        @pl.when(y == 0)
        def _():
            out_l[...] = src[...].astype(BF16)

        @pl.when(y > 0)
        def _():
            e_ahead.wait_recv()
            e_beside.start()
            a_re, a_im = sandwich(trans, in_e)
            out_l[0] = (src[0] + a_re).astype(BF16)
            out_l[1] = (src[1] + a_im).astype(BF16)

        @pl.when(y < 3)
        def _():
            e_ahead.start()

        @pl.when(y > 0)
        def _():
            e_beside.wait_send()

        @pl.when(y < 3)
        def _():
            e_ahead.wait_send()

    wait_recv(5, q_r)
    unpack(q_r, out_r)
    for slot, buffer in enumerate((s_gl, s_wl, s_gr, s_wr, o_l, o_r)):
        wait_send(slot, buffer)


def body(green_lesser, screened_lesser, green_retarded, screened_retarded, left_green, coupling):
    blocks = [a[0, 0] for a in (green_lesser, screened_lesser, green_retarded, screened_retarded, left_green)]
    forward, back = tables()
    block = blocks[0].shape
    vmem = pl.BlockSpec(memory_space=pltpu.VMEM)
    chunks = pltpu.VMEM((NE, 16, 128), BF16)
    spectra = pltpu.VMEM((4, 2, LENGTH, 256), F32)
    whole = pltpu.VMEM(block, BF16)
    out_l, out_r = pl.pallas_call(
        kernel,
        out_shape=[jax.ShapeDtypeStruct(block, BF16)] * 2,
        in_specs=[vmem] * 8,
        out_specs=[vmem] * 2,
        scratch_shapes=[chunks] * 12
        + [pltpu.VMEM((NE * 16, 128), F32)] * 2
        + [spectra] * 3
        + [whole, whole, whole, pltpu.VMEM(block, F32), whole, whole, whole, whole]
        + [pltpu.SemaphoreType.DMA((6,)), pltpu.SemaphoreType.DMA((6,))]
        + [pltpu.SemaphoreType.DMA((4,)), pltpu.SemaphoreType.DMA((4,))],
        compiler_params=pltpu.CompilerParams(
            collective_id=0, has_side_effects=True, vmem_limit_bytes=48 * 2**20
        ),
    )(*blocks, coupling[0], jnp.asarray(forward), jnp.asarray(back))
    return out_l[None, None], out_r[None, None]


def solution(mesh):
    point = P("energy", "space", None, None, None)
    return jax.shard_map(
        body,
        mesh=mesh,
        in_specs=(point,) * 5 + (P("space", None, None, None),),
        out_specs=(point, point),
        check_vma=False,
    )
```

```python
import functools
import math

import jax
import jax.numpy as jnp
import ml_dtypes
import numpy as np
from jax import lax
from jax.experimental import pallas as pl
from jax.experimental.pallas import tpu as pltpu
from jax.sharding import PartitionSpec as P

MESH = pl.DeviceIdType.MESH
BF16 = jnp.bfloat16
F32 = jnp.float32
NE = 64
LENGTH = 96
LAG = 32


def split_table(table):
    upper = table.astype(ml_dtypes.bfloat16)
    lower = (table - upper.astype(np.float64)).astype(ml_dtypes.bfloat16)
    return np.stack([upper, lower])


def tables():
    step = 2.0 * math.pi / LENGTH
    k = np.arange(LENGTH)
    n = np.arange(NE)
    angle = (k[:, None] * n[None, :] % LENGTH) * step
    forward = np.block([[np.cos(angle), np.sin(angle)], [-np.sin(angle), np.cos(angle)]])
    angle = ((n[:, None] + LAG) * k[None, :] % LENGTH) * step
    back = np.block([[np.cos(angle), -np.sin(angle)], [np.sin(angle), np.cos(angle)]]) / LENGTH
    return split_table(forward), split_table(back)


def dot(first, second):
    return jnp.dot(first, second, preferred_element_type=F32)


def dot_t(first, second):
    return lax.dot_general(first, second, (((1,), (1,)), ((), ())), preferred_element_type=F32)


def product(a_re, a_im, b_re, b_im):
    return dot(a_re, b_re) - dot(a_im, b_im), dot(a_re, b_im) + dot(a_im, b_re)


def adjoint(a_re, a_im, b_re, b_im):
    return dot_t(a_re, b_re) + dot_t(a_im, b_im), dot_t(a_im, b_re) - dot_t(a_re, b_im)


def sandwich(p_ref, s_ref):
    p_re, p_im = p_ref[0], p_ref[1]
    i_re, i_im = product(p_re, p_im, s_ref[0], s_ref[1])
    return adjoint(i_re.astype(BF16), i_im.astype(BF16), p_re, p_im)


def pack(src, dst):
    @pl.loop(0, 16)
    def _(b):
        for cb in range(2):
            re = src[0, pl.ds(16 * b, 16), 128 * cb : 128 * cb + 128].astype(F32)
            im = src[1, pl.ds(16 * b, 16), 128 * cb : 128 * cb + 128].astype(F32)
            for h in range(2):
                both = jnp.concatenate([re[8 * h : 8 * h + 8], im[8 * h : 8 * h + 8]], axis=0)
                dst[4 * b + 2 * h + cb, :, :] = both.astype(BF16)


def unpack(src, dst):
    @pl.loop(0, 16)
    def _(b):
        for cb in range(2):
            low = src[4 * b + cb].astype(F32)
            high = src[4 * b + 2 + cb].astype(F32)
            for part in range(2):
                rows = slice(8 * part, 8 * part + 8)
                both = jnp.concatenate([low[rows], high[rows]], axis=0)
                dst[part, pl.ds(16 * b, 16), 128 * cb : 128 * cb + 128] = both.astype(BF16)


def stage(received, wide):
    @pl.loop(0, 16)
    def _(i):
        wide[pl.ds(64 * i, 64), :] = received[pl.ds(4 * i, 4)].reshape(64, 128).astype(F32)


def gather_columns(wide, q):
    columns = []
    for s in (2 * q, 2 * q + 1):
        re = wide[pl.ds(s, NE, 16), :]
        im = wide[pl.ds(8 + s, NE, 16), :]
        columns.append(jnp.concatenate([re, im], axis=0))
    return jnp.concatenate(columns, axis=1).astype(BF16)


def spectrum(wide, forward, q):
    columns = gather_columns(wide, q)
    both = dot(forward[0], columns) + dot(forward[1], columns)
    return both[:LENGTH], both[LENGTH:]


def times(a, b):
    return a[0] * b[0] - a[1] * b[1], a[0] * b[1] + a[1] * b[0]


def back_to_energy(hat, back, wide, q):
    both = jnp.concatenate(hat, axis=0)
    upper = both.astype(BF16)
    lower = (both - upper.astype(F32)).astype(BF16)
    values = dot(back[0], upper) + dot(back[1], upper) + dot(back[0], lower)
    for i, s in enumerate((2 * q, 2 * q + 1)):
        wide[pl.ds(s, NE, 16), :] = values[:NE, 128 * i : 128 * i + 128]
        wide[pl.ds(8 + s, NE, 16), :] = values[NE:, 128 * i : 128 * i + 128]


def narrow(wide, dst):
    @pl.loop(0, 16)
    def _(i):
        dst[pl.ds(4 * i, 4)] = wide[pl.ds(64 * i, 64), :].reshape(4, 16, 128).astype(BF16)


def kernel(
    hbm_gl, hbm_wl, hbm_gr, hbm_wr, hbm_lg, hbm_cp, hbm_fwd, hbm_bwd, out_l, out_r,
    gl, wl, gr, wr, lg, cp, fwd, bwd,
    s_gl, s_wl, s_gr, s_wr, r_gl, r_wl, r_gr, r_wr, o_l, o_r, q_l, q_r,
    wide_a, wide_b, f_gl, f_wl, f_gr,
    sig, prop, trans, src, half, in_p, in_s, in_e,
    e_send, e_recv, s_send, s_recv, l_sem,
):
    me = lax.axis_index("energy")
    pos = lax.axis_index("space")
    y, core = pos // 2, pos % 2

    loads = [
        pltpu.make_async_copy(source, target, l_sem.at[i])
        for i, (source, target) in enumerate(
            (
                (hbm_gl, gl),
                (hbm_wl, wl),
                (hbm_gr, gr),
                (hbm_wr, wr),
                (hbm_lg, lg),
                (hbm_cp, cp),
                (hbm_fwd, fwd),
                (hbm_bwd, bwd),
            )
        )
    ]
    for load in loads:
        load.start()

    barrier = pltpu.get_barrier_semaphore()

    @pl.loop(1, NE)
    def _(s):
        pl.semaphore_signal(barrier, inc=1, device_id={"energy": lax.rem(me + s, NE)}, device_id_type=MESH)

    @pl.loop(1, 8)
    def _(s):
        pl.semaphore_signal(barrier, inc=1, device_id={"space": lax.rem(pos + s, 8)}, device_id_type=MESH)

    for load, source, target in zip(loads, (gl, wl, gr, wr), (s_gl, s_wl, s_gr, s_wr)):
        load.wait()
        pack(source, target)
    for load in loads[4:]:
        load.wait()
    pl.semaphore_wait(barrier, NE - 1 + 7)

    def exchange(slot, *pairs):
        @pl.loop(1, NE)
        def _(s):
            peer = lax.rem(me + s, NE)
            for i, (source, target) in enumerate(pairs):
                pltpu.make_async_remote_copy(
                    src_ref=source.at[peer],
                    dst_ref=target.at[me],
                    send_sem=e_send.at[slot + i],
                    recv_sem=e_recv.at[slot + i],
                    device_id={"energy": peer},
                    device_id_type=MESH,
                ).start()

        for source, target in pairs:
            target[me] = source[me]

    def wait_recv(slot, buffer):
        pltpu.make_async_copy(buffer.at[pl.ds(0, NE - 1)], buffer.at[pl.ds(0, NE - 1)], e_recv.at[slot]).wait()

    def wait_send(slot, buffer):
        pltpu.make_async_copy(buffer.at[pl.ds(0, NE - 1)], buffer.at[pl.ds(0, NE - 1)], e_send.at[slot]).wait()

    def to_space(slot, source, target, where):
        return pltpu.make_async_remote_copy(
            src_ref=source,
            dst_ref=target,
            send_sem=s_send.at[slot],
            recv_sem=s_recv.at[slot],
            device_id={"space": where},
            device_id_type=MESH,
        )

    exchange(0, (s_gl, r_gl), (s_wl, r_wl))
    exchange(2, (s_gr, r_gr))

    p_re, p_im = product(lg[0], lg[1], cp[0], cp[1])
    prop[0] = p_re.astype(BF16)
    prop[1] = p_im.astype(BF16)
    p_over = to_space(0, prop, in_p, lax.rem(pos + 1, 8))

    @pl.when(core == 0)
    def _():
        p_over.start()
        p_over.wait_send()

    @pl.when(core == 1)
    def _():
        p_over.wait_recv()
        t_re, t_im = product(prop[0], prop[1], in_p[0], in_p[1])
        trans[0] = t_re.astype(BF16)
        trans[1] = t_im.astype(BF16)

    wait_recv(0, r_gl)
    wait_recv(1, r_wl)
    stage(r_gl, wide_a)
    stage(r_wl, wide_b)
    for q in range(4):
        f_gl[q, 0], f_gl[q, 1] = spectrum(wide_a, fwd, q)
        f_wl[q, 0], f_wl[q, 1] = spectrum(wide_b, fwd, q)
    for q in range(4):
        hat = times((f_gl[q, 0], f_gl[q, 1]), (f_wl[q, 0], f_wl[q, 1]))
        back_to_energy(hat, bwd, wide_a, q)
    narrow(wide_a, o_l)
    exchange(4, (o_l, q_l))
    exchange(3, (s_wr, r_wr))

    wait_recv(2, r_gr)
    stage(r_gr, wide_a)
    for q in range(4):
        f_gr[q, 0], f_gr[q, 1] = spectrum(wide_a, fwd, q)

    wait_recv(4, q_l)
    unpack(q_l, sig)
    h_re, h_im = product(lg[0], lg[1], sig[0], sig[1])
    half[0] = h_re.astype(BF16)
    half[1] = h_im.astype(BF16)
    src[0], src[1] = adjoint(half[0], half[1], lg[0], lg[1])
    s_over = to_space(1, half, in_s, lax.rem(pos + 1, 8))

    @pl.when(core == 0)
    def _():
        half[0] = src[0].astype(BF16)
        half[1] = src[1].astype(BF16)
        s_over.start()

    @pl.when(core == 1)
    def _():
        s_over.wait_recv()
        a_re, a_im = sandwich(prop, in_s)
        src[0] += a_re
        src[1] += a_im

    def finish_retarded():
        wait_recv(3, r_wr)
        stage(r_wr, wide_b)
        for q in range(4):
            w_r = spectrum(wide_b, fwd, q)
            w_l = (f_wl[q, 0], f_wl[q, 1])
            first = times((f_gr[q, 0], f_gr[q, 1]), (w_l[0] + w_r[0], w_l[1] + w_r[1]))
            second = times((f_gl[q, 0], f_gl[q, 1]), w_r)
            back_to_energy((first[0] + second[0], first[1] + second[1]), bwd, wide_a, q)
        narrow(wide_a, o_r)
        exchange(5, (o_r, q_r))

    finish_retarded()

    e_ahead = to_space(2, out_l, in_e, lax.rem(pos + 2, 8))
    e_beside = to_space(3, in_e, in_e, lax.rem(pos + 7, 8))

    @pl.when(core == 0)
    def _():
        s_over.wait_send()

        @pl.when(y == 0)
        def _():
            out_l[...] = src[...].astype(BF16)

        @pl.when(y > 0)
        def _():
            e_beside.wait_recv()
            a_re, a_im = sandwich(prop, in_e)
            out_l[0] = (src[0] + a_re).astype(BF16)
            out_l[1] = (src[1] + a_im).astype(BF16)

    @pl.when(core == 1)
    def _():
        @pl.when(y == 0)
        def _():
            out_l[...] = src[...].astype(BF16)

        @pl.when(y > 0)
        def _():
            e_ahead.wait_recv()
            e_beside.start()
            a_re, a_im = sandwich(trans, in_e)
            out_l[0] = (src[0] + a_re).astype(BF16)
            out_l[1] = (src[1] + a_im).astype(BF16)

        @pl.when(y < 3)
        def _():
            e_ahead.start()

        @pl.when(y > 0)
        def _():
            e_beside.wait_send()

        @pl.when(y < 3)
        def _():
            e_ahead.wait_send()

    wait_recv(5, q_r)
    unpack(q_r, out_r)
    for slot, buffer in enumerate((s_gl, s_wl, s_gr, s_wr, o_l, o_r)):
        wait_send(slot, buffer)


def body(green_lesser, screened_lesser, green_retarded, screened_retarded, left_green, coupling):
    blocks = [a[0, 0] for a in (green_lesser, screened_lesser, green_retarded, screened_retarded, left_green)]
    forward, back = tables()
    block = blocks[0].shape
    vmem = pl.BlockSpec(memory_space=pltpu.VMEM)
    chunks = pltpu.VMEM((NE, 16, 128), BF16)
    spectra = pltpu.VMEM((4, 2, LENGTH, 256), F32)
    whole = pltpu.VMEM(block, BF16)
    out_l, out_r = pl.pallas_call(
        kernel,
        out_shape=[jax.ShapeDtypeStruct(block, BF16)] * 2,
        in_specs=[pl.BlockSpec(memory_space=pltpu.HBM)] * 8,
        out_specs=[vmem] * 2,
        scratch_shapes=[whole] * 6
        + [pltpu.VMEM(forward.shape, BF16), pltpu.VMEM(back.shape, BF16)]
        + [chunks] * 12
        + [pltpu.VMEM((NE * 16, 128), F32)] * 2
        + [spectra] * 3
        + [whole, whole, whole, pltpu.VMEM(block, F32), whole, whole, whole, whole]
        + [pltpu.SemaphoreType.DMA((6,)), pltpu.SemaphoreType.DMA((6,))]
        + [pltpu.SemaphoreType.DMA((4,)), pltpu.SemaphoreType.DMA((4,)), pltpu.SemaphoreType.DMA((8,))],
        compiler_params=pltpu.CompilerParams(
            collective_id=0, has_side_effects=True, vmem_limit_bytes=63 * 2**20
        ),
    )(*blocks, coupling[0], jnp.asarray(forward), jnp.asarray(back))
    return out_l[None, None], out_r[None, None]


def solution(mesh):
    point = P("energy", "space", None, None, None)
    return jax.shard_map(
        body,
        mesh=mesh,
        in_specs=(point,) * 5 + (P("space", None, None, None),),
        out_specs=(point, point),
        check_vma=False,
    )
```

```python
import functools
import math

import jax
import jax.numpy as jnp
import ml_dtypes
import numpy as np
from jax import lax
from jax.experimental import pallas as pl
from jax.experimental.pallas import tpu as pltpu
from jax.sharding import PartitionSpec as P

MESH = pl.DeviceIdType.MESH
BF16 = jnp.bfloat16
F32 = jnp.float32
NE = 64
LENGTH = 96
LAG = 32


def split_table(table):
    upper = table.astype(ml_dtypes.bfloat16)
    lower = (table - upper.astype(np.float64)).astype(ml_dtypes.bfloat16)
    return np.stack([upper, lower])


def tables():
    step = 2.0 * math.pi / LENGTH
    k = np.arange(LENGTH)
    n = np.arange(NE)
    angle = (k[:, None] * n[None, :] % LENGTH) * step
    forward = np.block([[np.cos(angle), np.sin(angle)], [-np.sin(angle), np.cos(angle)]])
    angle = ((n[:, None] + LAG) * k[None, :] % LENGTH) * step
    back = np.block([[np.cos(angle), -np.sin(angle)], [np.sin(angle), np.cos(angle)]]) / LENGTH
    return split_table(forward), split_table(back)


def dot(first, second):
    return jnp.dot(first, second, preferred_element_type=F32)


def dot_t(first, second):
    return lax.dot_general(first, second, (((1,), (1,)), ((), ())), preferred_element_type=F32)


def product(a_re, a_im, b_re, b_im):
    return dot(a_re, b_re) - dot(a_im, b_im), dot(a_re, b_im) + dot(a_im, b_re)


def adjoint(a_re, a_im, b_re, b_im):
    return dot_t(a_re, b_re) + dot_t(a_im, b_im), dot_t(a_im, b_re) - dot_t(a_re, b_im)


def sandwich(p_ref, s_ref):
    p_re, p_im = p_ref[0], p_ref[1]
    i_re, i_im = product(p_re, p_im, s_ref[0], s_ref[1])
    return adjoint(i_re.astype(BF16), i_im.astype(BF16), p_re, p_im)


def pack(src, dst):
    @pl.loop(0, 16)
    def _(b):
        for cb in range(2):
            re = src[0, pl.ds(16 * b, 16), 128 * cb : 128 * cb + 128].astype(F32)
            im = src[1, pl.ds(16 * b, 16), 128 * cb : 128 * cb + 128].astype(F32)
            for h in range(2):
                both = jnp.concatenate([re[8 * h : 8 * h + 8], im[8 * h : 8 * h + 8]], axis=0)
                dst[4 * b + 2 * h + cb, :, :] = both.astype(BF16)


def unpack(src, dst):
    @pl.loop(0, 16)
    def _(b):
        for cb in range(2):
            low = src[4 * b + cb].astype(F32)
            high = src[4 * b + 2 + cb].astype(F32)
            for part in range(2):
                rows = slice(8 * part, 8 * part + 8)
                both = jnp.concatenate([low[rows], high[rows]], axis=0)
                dst[part, pl.ds(16 * b, 16), 128 * cb : 128 * cb + 128] = both.astype(BF16)


def stage(received, wide):
    @pl.loop(0, 16)
    def _(i):
        wide[pl.ds(64 * i, 64), :] = received[pl.ds(4 * i, 4)].reshape(64, 128).astype(F32)


def gather_columns(wide, q):
    columns = []
    for s in (2 * q, 2 * q + 1):
        re = wide[pl.ds(s, NE, 16), :]
        im = wide[pl.ds(8 + s, NE, 16), :]
        columns.append(jnp.concatenate([re, im], axis=0))
    return jnp.concatenate(columns, axis=1).astype(BF16)


def spectrum(wide, forward, q):
    columns = gather_columns(wide, q)
    both = dot(forward[0], columns) + dot(forward[1], columns)
    return both[:LENGTH], both[LENGTH:]


def times(a, b):
    return a[0] * b[0] - a[1] * b[1], a[0] * b[1] + a[1] * b[0]


def back_to_energy(hat, back, wide, q):
    both = jnp.concatenate(hat, axis=0)
    upper = both.astype(BF16)
    lower = (both - upper.astype(F32)).astype(BF16)
    values = dot(back[0], upper) + dot(back[1], upper) + dot(back[0], lower)
    for i, s in enumerate((2 * q, 2 * q + 1)):
        wide[pl.ds(s, NE, 16), :] = values[:NE, 128 * i : 128 * i + 128]
        wide[pl.ds(8 + s, NE, 16), :] = values[NE:, 128 * i : 128 * i + 128]


def narrow(wide, dst):
    @pl.loop(0, 16)
    def _(i):
        dst[pl.ds(4 * i, 4)] = wide[pl.ds(64 * i, 64), :].reshape(4, 16, 128).astype(BF16)


def kernel(
    hbm_gl, hbm_wl, hbm_gr, hbm_wr, hbm_lg, hbm_cp, hbm_fwd, hbm_bwd, out_l, out_r,
    gl, wl, gr, wr, lg, cp, fwd, bwd,
    s_gl, s_wl, s_gr, s_wr, r_gl, r_wl, r_gr, r_wr, o_l, o_r, q_l, q_r,
    wide_a, wide_b, f_gl, f_wl, f_gr,
    sig, prop, trans, src, half, in_p, in_s, in_e,
    e_send, e_recv, s_send, s_recv, l_sem,
):
    me = lax.axis_index("energy")
    pos = lax.axis_index("space")
    y, core = pos // 2, pos % 2

    loads = [
        pltpu.make_async_copy(source, target, l_sem.at[i])
        for i, (source, target) in enumerate(
            (
                (hbm_gl, gl),
                (hbm_wl, wl),
                (hbm_gr, gr),
                (hbm_wr, wr),
                (hbm_lg, lg),
                (hbm_cp, cp),
                (hbm_fwd, fwd),
                (hbm_bwd, bwd),
            )
        )
    ]
    for load in loads:
        load.start()

    barrier = pltpu.get_barrier_semaphore()

    @pl.loop(1, NE)
    def _(s):
        pl.semaphore_signal(barrier, inc=1, device_id={"energy": lax.rem(me + s, NE)}, device_id_type=MESH)

    @pl.loop(1, 8)
    def _(s):
        pl.semaphore_signal(barrier, inc=1, device_id={"space": lax.rem(pos + s, 8)}, device_id_type=MESH)

    for load, source, target in zip(loads, (gl, wl, gr, wr), (s_gl, s_wl, s_gr, s_wr)):
        load.wait()
        pack(source, target)
    for load in loads[4:]:
        load.wait()
    pl.semaphore_wait(barrier, NE - 1 + 7)

    def exchange(slot, *pairs):
        @pl.loop(1, NE)
        def _(s):
            peer = lax.rem(me + s, NE)
            for i, (source, target) in enumerate(pairs):
                pltpu.make_async_remote_copy(
                    src_ref=source.at[peer],
                    dst_ref=target.at[me],
                    send_sem=e_send.at[slot + i],
                    recv_sem=e_recv.at[slot + i],
                    device_id={"energy": peer},
                    device_id_type=MESH,
                ).start()

        for source, target in pairs:
            target[me] = source[me]

    def wait_recv(slot, buffer):
        pltpu.make_async_copy(buffer.at[pl.ds(0, NE - 1)], buffer.at[pl.ds(0, NE - 1)], e_recv.at[slot]).wait()

    def wait_send(slot, buffer):
        pltpu.make_async_copy(buffer.at[pl.ds(0, NE - 1)], buffer.at[pl.ds(0, NE - 1)], e_send.at[slot]).wait()

    def to_space(slot, source, target, where):
        return pltpu.make_async_remote_copy(
            src_ref=source,
            dst_ref=target,
            send_sem=s_send.at[slot],
            recv_sem=s_recv.at[slot],
            device_id={"space": where},
            device_id_type=MESH,
        )

    exchange(0, (s_gl, r_gl), (s_wl, r_wl))
    exchange(2, (s_gr, r_gr))

    p_re, p_im = product(lg[0], lg[1], cp[0], cp[1])
    prop[0] = p_re.astype(BF16)
    prop[1] = p_im.astype(BF16)
    p_over = to_space(0, prop, in_p, lax.rem(pos + 1, 8))

    @pl.when(core == 0)
    def _():
        p_over.start()
        p_over.wait_send()

    @pl.when(core == 1)
    def _():
        p_over.wait_recv()
        t_re, t_im = product(prop[0], prop[1], in_p[0], in_p[1])
        trans[0] = t_re.astype(BF16)
        trans[1] = t_im.astype(BF16)

    wait_recv(0, r_gl)
    wait_recv(1, r_wl)
    stage(r_gl, wide_a)
    stage(r_wl, wide_b)
    for q in range(4):
        f_gl[q, 0], f_gl[q, 1] = spectrum(wide_a, fwd, q)
        f_wl[q, 0], f_wl[q, 1] = spectrum(wide_b, fwd, q)
    for q in range(4):
        hat = times((f_gl[q, 0], f_gl[q, 1]), (f_wl[q, 0], f_wl[q, 1]))
        back_to_energy(hat, bwd, wide_a, q)
    narrow(wide_a, o_l)
    exchange(4, (o_l, q_l))
    exchange(3, (s_wr, r_wr))

    wait_recv(2, r_gr)
    stage(r_gr, wide_a)
    for q in range(4):
        f_gr[q, 0], f_gr[q, 1] = spectrum(wide_a, fwd, q)

    wait_recv(4, q_l)
    unpack(q_l, sig)
    h_re, h_im = product(lg[0], lg[1], sig[0], sig[1])
    half[0] = h_re.astype(BF16)
    half[1] = h_im.astype(BF16)
    src[0], src[1] = adjoint(half[0], half[1], lg[0], lg[1])
    s_over = to_space(1, half, in_s, lax.rem(pos + 1, 8))

    @pl.when(core == 0)
    def _():
        half[0] = src[0].astype(BF16)
        half[1] = src[1].astype(BF16)
        s_over.start()

    @pl.when(core == 1)
    def _():
        s_over.wait_recv()
        a_re, a_im = sandwich(prop, in_s)
        src[0] += a_re
        src[1] += a_im

    def finish_retarded():
        wait_recv(3, r_wr)
        stage(r_wr, wide_b)
        for q in range(4):
            w_r = spectrum(wide_b, fwd, q)
            w_l = (f_wl[q, 0], f_wl[q, 1])
            first = times((f_gr[q, 0], f_gr[q, 1]), (w_l[0] + w_r[0], w_l[1] + w_r[1]))
            second = times((f_gl[q, 0], f_gl[q, 1]), w_r)
            back_to_energy((first[0] + second[0], first[1] + second[1]), bwd, wide_a, q)
        narrow(wide_a, o_r)
        exchange(5, (o_r, q_r))

    e_ahead = to_space(2, out_l, in_e, lax.rem(pos + 2, 8))
    e_beside = to_space(3, in_e, in_e, lax.rem(pos + 7, 8))

    @pl.when(y == 0)
    def _():
        out_l[...] = src[...].astype(BF16)

        @pl.when(core == 1)
        def _():
            e_ahead.start()

    finish_retarded()


    @pl.when(core == 0)
    def _():
        s_over.wait_send()

        @pl.when(y > 0)
        def _():
            e_beside.wait_recv()
            a_re, a_im = sandwich(prop, in_e)
            out_l[0] = (src[0] + a_re).astype(BF16)
            out_l[1] = (src[1] + a_im).astype(BF16)

    @pl.when(core == 1)
    def _():
        @pl.when(y > 0)
        def _():
            e_ahead.wait_recv()
            e_beside.start()
            a_re, a_im = sandwich(trans, in_e)
            out_l[0] = (src[0] + a_re).astype(BF16)
            out_l[1] = (src[1] + a_im).astype(BF16)

        @pl.when(jnp.logical_and(y > 0, y < 3))
        def _():
            e_ahead.start()

        @pl.when(y > 0)
        def _():
            e_beside.wait_send()

        @pl.when(y < 3)
        def _():
            e_ahead.wait_send()

    wait_recv(5, q_r)
    unpack(q_r, out_r)
    for slot, buffer in enumerate((s_gl, s_wl, s_gr, s_wr, o_l, o_r)):
        wait_send(slot, buffer)


def body(green_lesser, screened_lesser, green_retarded, screened_retarded, left_green, coupling):
    blocks = [a[0, 0] for a in (green_lesser, screened_lesser, green_retarded, screened_retarded, left_green)]
    forward, back = tables()
    block = blocks[0].shape
    vmem = pl.BlockSpec(memory_space=pltpu.VMEM)
    chunks = pltpu.VMEM((NE, 16, 128), BF16)
    spectra = pltpu.VMEM((4, 2, LENGTH, 256), F32)
    whole = pltpu.VMEM(block, BF16)
    out_l, out_r = pl.pallas_call(
        kernel,
        out_shape=[jax.ShapeDtypeStruct(block, BF16)] * 2,
        in_specs=[pl.BlockSpec(memory_space=pltpu.HBM)] * 8,
        out_specs=[vmem] * 2,
        scratch_shapes=[whole] * 6
        + [pltpu.VMEM(forward.shape, BF16), pltpu.VMEM(back.shape, BF16)]
        + [chunks] * 12
        + [pltpu.VMEM((NE * 16, 128), F32)] * 2
        + [spectra] * 3
        + [whole, whole, whole, pltpu.VMEM(block, F32), whole, whole, whole, whole]
        + [pltpu.SemaphoreType.DMA((6,)), pltpu.SemaphoreType.DMA((6,))]
        + [pltpu.SemaphoreType.DMA((4,)), pltpu.SemaphoreType.DMA((4,)), pltpu.SemaphoreType.DMA((8,))],
        compiler_params=pltpu.CompilerParams(
            collective_id=0, has_side_effects=True, vmem_limit_bytes=63 * 2**20
        ),
    )(*blocks, coupling[0], jnp.asarray(forward), jnp.asarray(back))
    return out_l[None, None], out_r[None, None]


def solution(mesh):
    point = P("energy", "space", None, None, None)
    return jax.shard_map(
        body,
        mesh=mesh,
        in_specs=(point,) * 5 + (P("space", None, None, None),),
        out_specs=(point, point),
        check_vma=False,
    )
```
